32 devices in a mesh: segment: 4 (over y, x), tile: 8 (over z, core).
Axes of the slice: x: 2, y: 2, z: 4, core: 2. Of those that a mesh axis runs over, the one named last changes fastest.
Arguments:
- latent_clips: bfloat16 [4, 2, 32, 128, 128], P('segment', None, 'tile'), may hold values from -1.5 to 1.5
- augment_noise: bfloat16 [4, 4, 2, 32, 128, 128], P('segment', None, None, 'tile'), may hold values from -3.59375 to 3.59375
- section_weights: bfloat16 [4, 1152, 128], P('segment'), may hold values from -2 to 2
- frame_mixing: float32 [6, 128], replicated, may hold values from 0.1 to 0.9
- step_embed: float32 [6, 128], replicated, may hold values from -3 to 3
Outputs:
- sampled_clips: bfloat16 [4, 2, 32, 128, 128], P('segment', None, 'tile')
The draws below stay inside these ranges and needn't reach their ends.
All inputs are finite; a program needn't handle non-finite values.
Results may differ from the reference program's by a relative error of at most 0.017.
Values may be sent and summed in bfloat16 or wider, within the bound.
No kernel may reach another device: no remote copies, remote signals or barrier semaphores. Data moves between devices by JAX's collectives and lax.ppermute only.
A program may use at most 64 MiB of HBM per device.

```python
import math
import jax
import jax.numpy as jnp
from jax import lax

C = 128
FRAMES = 2
COLS = 128
STEPS_BASE = 3
STEPS_SR = 1
NSTEP = 6
MB = 4
ROWS = 32
N_SEGMENT = 4


def draw_section_weights(key, part):
    shape = (N_SEGMENT, 3, 3, C, C)
    base = jnp.clip(jax.random.normal(key, shape, jnp.float32), -3.5, 3.5)
    row_gain = jnp.array([1.0, 0.25, 0.6], jnp.float32)
    scaled = base * row_gain[None, :, None, None, None] * (4.0 / math.sqrt(3.0 * C))
    return scaled.reshape(N_SEGMENT, 9 * C, C).astype(jnp.bfloat16)


def block_levels(own_key, extent, cuts, smallest, largest):
    level, own = 1.0, jax.random.fold_in(own_key, 6)
    for position, blocks in cuts:
        heights = jnp.exp(jax.random.uniform(jax.random.fold_in(own, position), (blocks,), jnp.float32, smallest / len(cuts), largest / len(cuts)))
        level = level * jnp.repeat(heights, extent[position] // blocks).reshape([-1 if axis == position else 1 for axis in range(len(extent))])
    return level


def centred(rng, shape, width, reach, shards=(), dtype=jnp.bfloat16):
    loudness = block_levels(rng, shape, shards, -0.22, 0.18) if shards else 1.0
    values = jax.random.normal(rng, shape, jnp.float32) * width * loudness
    return jnp.minimum(jnp.maximum(values, -reach), reach).astype(dtype)


def setup_inputs(seed: int = 0) -> dict:
    key_of = jax.random.split(jax.random.key(seed), 6)
    latent_clips = centred(key_of[0], (MB, FRAMES, ROWS, COLS, C), 0.25, 1.5, ((0, 4), (2, 8)))
    augment_noise = centred(key_of[1], (N_SEGMENT, MB, FRAMES, ROWS, COLS, C), 0.6, 3.59375, ((0, 4), (3, 8)))
    section_weights = draw_section_weights(jax.random.fold_in(key_of[5], 71), 0)
    frame_mixing = jnp.clip(jax.random.uniform(key_of[3], (NSTEP, C), jnp.float32, 0.1, 0.9), 0.1, 0.9)
    step_embed = centred(key_of[4], (NSTEP, C), 0.5, 3.0, (), jnp.float32)
    return {"latent_clips": latent_clips, "augment_noise": augment_noise, "section_weights": section_weights, "frame_mixing": frame_mixing, "step_embed": step_embed}


norm_eps = 1e-06
keep_coef = 0.9
update_coef = 0.5
noise_coef = 0.5

def conv_step(latent, weight, mixing, embedding):
    latent_f32 = latent.astype(jnp.float32)
    frame_mean = lax.optimization_barrier(jnp.mean(latent_f32, axis=0, keepdims=True))
    mixed = (latent_f32 + mixing * (frame_mean - latent_f32)).astype(jnp.bfloat16)
    padded = jnp.pad(mixed, ((0, 0), (1, 1), (1, 1), (0, 0)))
    row_count = mixed.shape[1]
    col_count = mixed.shape[2]
    patches = jnp.concatenate([padded[:, row_off:row_off + row_count, col_off:col_off + col_count, :] for row_off in range(3) for col_off in range(3)], axis=-1)
    conv_out = jnp.dot(patches.reshape(-1, patches.shape[-1]), weight, preferred_element_type=jnp.float32).reshape(latent.shape) + embedding
    scaled = conv_out * lax.rsqrt(lax.optimization_barrier(jnp.mean(conv_out * conv_out, axis=-1, keepdims=True)) + norm_eps)
    return (keep_coef * latent_f32 + update_coef * jax.nn.silu(scaled)).astype(jnp.bfloat16)

def reference(latent_clips, augment_noise, section_weights, frame_mixing, step_embed):
    finished = []
    for clip_index in range(MB):
        latent = latent_clips[clip_index]
        step_index = 0
        for section in range(N_SEGMENT):
            latent = (latent.astype(jnp.float32) + noise_coef * augment_noise[section, clip_index].astype(jnp.float32)).astype(jnp.bfloat16)
            count = STEPS_BASE if section == 0 else STEPS_SR
            for repeat in range(count):
                latent = conv_step(latent, section_weights[section], frame_mixing[step_index], step_embed[step_index])
                step_index = step_index + 1
        finished.append(latent)
    return jnp.stack(finished)
```

```python
import functools

import jax
import jax.numpy as jnp
from jax import lax
from jax.experimental import pallas as pl
from jax.experimental.pallas import tpu as pltpu
from jax.sharding import PartitionSpec as P

STEPS_BASE = 3
STEPS_SR = 1

norm_eps = 1e-06
keep_coef = 0.9
update_coef = 0.5
noise_coef = 0.5

HALO = 3
CHUNK = 64
SUBLANES = 8
f32 = jnp.float32
bf16 = jnp.bfloat16


def add_noise(latent, noise_piece):
    return (latent.astype(f32) + noise_coef * noise_piece.astype(f32)).astype(bf16)


def fill_taps(taps_ref, weight_ref, start):
    count, chans = weight_ref.shape
    row = taps_ref.shape[0] // 4
    weight = weight_ref[...]
    taps_ref[start : start + count, :chans] = weight
    taps_ref[row + start : row + start + count, chans:] = weight


def build_taps(taps_ref, core, place, mine_ref, other_ref):
    _, half, chans = mine_ref.shape
    row = taps_ref.shape[0] // 4
    taps_ref[3 * row :, :chans] = jnp.zeros((row, chans), bf16)
    taps_ref[:row, chans:] = jnp.zeros((row, chans), bf16)
    for flag, low, high in ((1 - core, mine_ref, other_ref), (core, other_ref, mine_ref)):

        @pl.when(flag == 1)
        def _(low=low, high=high):
            fill_taps(taps_ref, low.at[place], 0)
            fill_taps(taps_ref, high.at[place], half)


def taps_kernel(first, flags_ref, mine_ref, other_ref, taps_ref):
    for k in range(taps_ref.shape[0]):
        build_taps(taps_ref.at[k], 1 - flags_ref[2], flags_ref[3 + first + k], mine_ref, other_ref)


def make_taps(first, last, flags, mine, other):
    _, half, chans = mine.shape
    vmem = pl.BlockSpec(memory_space=pltpu.VMEM)
    return pl.pallas_call(
        functools.partial(taps_kernel, first),
        out_shape=jax.ShapeDtypeStruct((last - first, half // 3 * 8, 2 * chans), bf16),
        in_specs=[pl.BlockSpec(memory_space=pltpu.SMEM), vmem, vmem],
        out_specs=vmem,
        compiler_params=pltpu.CompilerParams(vmem_limit_bytes=16 * 1024 * 1024),
        cost_estimate=pl.CostEstimate(flops=0, bytes_accessed=(last - first) * half * 16 * chans, transcendentals=0),
    )(flags, mine, other)


def store_mixed(mixed_ref, state_ref, row, mixing, flag):
    frames, _, cols, chans = state_ref.shape
    first, second = [state_ref[frame, row] for frame in range(frames)]
    delta = (second - first) * mixing
    spot = lax.broadcasted_iota(jnp.int32, (SUBLANES, chans), 0)
    for index, mixed in enumerate((first + delta, second - delta)):
        if flag is not None:
            mixed = mixed * flag
        here = pl.ds(index * cols, cols)
        left, right = pltpu.roll(mixed, 1, 0), pltpu.roll(mixed, cols - 1, 0)
        left = jnp.concatenate([jnp.where(spot == 0, 0.0, left[:SUBLANES]), left[SUBLANES:]], axis=0)
        rest = cols - SUBLANES
        right = jnp.concatenate([right[:rest], jnp.where(spot == SUBLANES - 1, 0.0, right[rest:])], axis=0)
        mixed_ref[row, here, :chans] = left.astype(bf16)
        mixed_ref[row, here, chans : 2 * chans] = mixed.astype(bf16)
        mixed_ref[row, here, 2 * chans :] = right.astype(bf16)


def place_halos(even, buffer_ref, off_ref, on_ref, above, below):
    width = off_ref.shape[1]
    for flag, upper, lower in ((even, off_ref, on_ref), (1 - even, on_ref, off_ref)):

        @pl.when(flag == 1)
        def _(upper=upper, lower=lower):
            buffer_ref[:, above : above + width] = upper[...].astype(buffer_ref.dtype)
            buffer_ref[:, below : below + width] = lower[...].astype(buffer_ref.dtype)


def steps_kernel(
    first_step, sections, rows, noise_widths, sends, flags_ref, own_ref, first_ref, second_ref, per_step_ref, *rest
):
    total_rows = rows + 2 * HALO
    rest = list(rest)
    on_ref, off_ref = (first_ref, second_ref) if sends else (second_ref, first_ref)
    if sends:
        mine_ref, other_ref = rest.pop(0), rest.pop(0)
    else:
        taps_ref = rest.pop(0)
    noises = {k: rest.pop(0) for k, width in enumerate(noise_widths) if width is not None}
    wide = [k for k, width in enumerate(noise_widths) if width]
    if wide:
        noise_on_ref, noise_off_ref = rest.pop(0), rest.pop(0)
    out_ref = rest.pop(0)
    if sends:
        send_off_ref, send_on_ref = rest.pop(0), rest.pop(0)
    state_ref, mixed_ref, conv_ref = rest[:3]
    rest = rest[3:]
    if sends:
        taps_ref = rest.pop(0)
        build_taps(taps_ref.at[0], 1 - flags_ref[2], flags_ref[3], mine_ref, other_ref)
    else:
        rows_ref, sem = rest.pop(0), rest.pop(0)
    buffers = dict(zip(wide, rest))
    frames, _, cols, chans = own_ref.shape
    up_flag = flags_ref[0].astype(f32)
    down_flag = flags_ref[1].astype(f32)
    even = flags_ref[2]
    place_halos(even, state_ref, off_ref, on_ref, 0, HALO + rows)
    start = 0
    for step in wide:
        width = noise_widths[step]
        part = pl.ds(start, width)
        place_halos(
            even, buffers[step], noise_off_ref.at[:, part], noise_on_ref.at[:, part], HALO - width, HALO + rows
        )
        start += width
    def flag_of(row):
        if row < HALO:
            return up_flag
        if row >= HALO + rows:
            return down_flag
        return None

    def is_own(row):
        return HALO <= row < HALO + rows

    def mixing_of(step):
        return per_step_ref[first_step + step : first_step + step + 1, :]

    def first_mix(row):
        if is_own(row):
            for frame in range(frames):
                state_ref[frame, row] = own_ref[frame, row - HALO].astype(f32)
        store_mixed(mixed_ref.at[0], state_ref, row, mixing_of(0), flag_of(row))

    pixels = frames * cols

    def convolve(step, base, slot):
        source = mixed_ref.at[step % 2]
        taps = taps_ref.at[sections[step]]
        for frame in range(frames):
            here = pl.ds(frame * cols, cols)
            patches = jnp.concatenate([source[base + i, here] for i in range(4)], axis=1)
            conv_ref[pl.ds(slot * pixels + frame * cols, cols), :] = jnp.dot(
                patches, taps[...], preferred_element_type=f32
            )

    def update(step, base, slot):
        place = per_step_ref.shape[0] // 2 + first_step + step
        embed = per_step_ref[place : place + 1, :]
        last = step == HALO - 1
        for j in range(2):
            row = base + 1 + j
            for frame in range(frames):
                for spot in range(0, cols, CHUNK):
                    here = pl.ds(spot, CHUNK)
                    part = conv_ref[pl.ds(slot * pixels + frame * cols + spot, CHUNK), j * chans : (j + 1) * chans] + embed
                    mean = jnp.sum(part * part, axis=1, keepdims=True) * (4.0 / chans)
                    half = part * lax.rsqrt(mean + 4.0 * norm_eps)
                    silu = half + half * jnp.tanh(half)
                    new = keep_coef * state_ref[frame, row, here] + update_coef * silu
                    if step in noises:
                        if is_own(row):
                            piece = noises[step][frame, row - HALO, here]
                        else:
                            piece = buffers[step][frame, row, here]
                        new = new + noise_coef * piece.astype(f32)
                    if last:
                        (out_ref if sends else rows_ref)[frame, row - HALO, here] = new.astype(bf16)
                    else:
                        state_ref[frame, row, here] = new
            if last and not sends:
                copy_row(row - HALO).start()
            if not last:
                store_mixed(mixed_ref.at[(step + 1) % 2], state_ref, row, mixing_of(step + 1), flag_of(row))

    def copy_row(row):
        return pltpu.make_async_copy(rows_ref.at[:, row], out_ref.at[:, row], sem.at[row])

    waiting = None
    mixed_rows = 0
    slot = 0
    for step in range(HALO):
        for base in range(step, total_rows - step - 2, 2):
            if step == 0:
                while mixed_rows < base + 4:
                    first_mix(mixed_rows)
                    mixed_rows += 1
            convolve(step, base, slot)
            if waiting is not None:
                update(*waiting)
            waiting = (step, base, slot)
            slot = 1 - slot
    update(*waiting)
    if not sends:
        for row in range(rows):
            copy_row(row).wait()
    if sends:
        for flag, off_rows, on_rows in ((even, 0, rows - HALO), (1 - even, rows - HALO, 0)):

            @pl.when(flag == 1)
            def _(off_rows=off_rows, on_rows=on_rows):
                send_off_ref[...] = out_ref[:, off_rows : off_rows + HALO]
                send_on_ref[...] = out_ref[:, on_rows : on_rows + HALO]


def run_steps(first_step, sections, noise_widths, sends, flags, own, off, on, per_step, taps, noises):
    frames, rows, cols, chans = own.shape
    depth = 9 * chans
    total = rows + 2 * HALO
    vmem = pl.BlockSpec(memory_space=pltpu.VMEM)
    halos = (on, off) if sends else (off, on)
    operands = (flags, own, *halos, per_step, *taps, *noises)
    outputs = sum(total - 2 * (k + 1) for k in range(HALO)) * frames * cols
    state = pltpu.VMEM((frames, total, cols, chans), f32)
    edges = pltpu.VMEM((frames, total, cols, chans), bf16)
    edge = jax.ShapeDtypeStruct((frames, HALO, cols, chans), bf16)
    whole = jax.ShapeDtypeStruct(own.shape, bf16)
    return pl.pallas_call(
        functools.partial(steps_kernel, first_step, sections, rows, noise_widths, sends),
        out_shape=(whole, edge, edge) if sends else whole,
        in_specs=[pl.BlockSpec(memory_space=pltpu.SMEM)] + [vmem] * (len(operands) - 1),
        out_specs=(vmem, vmem, vmem) if sends else pl.BlockSpec(memory_space=pl.ANY),
        scratch_shapes=[
            state,
            pltpu.VMEM((2, total, frames * cols, 3 * chans), bf16),
            pltpu.VMEM((2 * frames * cols, 2 * chans), f32),
        ]
        + (
            [pltpu.VMEM((1, depth // 3 * 4, 2 * chans), bf16)]
            if sends
            else [pltpu.VMEM(own.shape, bf16), pltpu.SemaphoreType.DMA((rows,))]
        )
        + [edges for width in noise_widths if width],
        compiler_params=pltpu.CompilerParams(vmem_limit_bytes=40 * 1024 * 1024),
        cost_estimate=pl.CostEstimate(
            flops=2 * outputs * depth * chans, bytes_accessed=4 * own.size, transcendentals=outputs * chans
        ),
    )(*operands)


def off_swap(value):
    count = lax.axis_size("tile")
    return lax.ppermute(value, "tile", [p for i in range(1, count - 1, 2) for p in ((i, i + 1), (i + 1, i))])


def on_swap(value):
    return lax.ppermute(value, "tile", [(i, i ^ 1) for i in range(lax.axis_size("tile"))])


def edges_to_send(top, bottom):
    even = lax.axis_index("tile") % 2 == 0
    return jnp.where(even, top, bottom), jnp.where(even, bottom, top)


def per_device(latent_clips, augment_noise, section_weights, frame_mixing, step_embed):
    segment = lax.axis_index("segment")
    tile = lax.axis_index("tile")
    segments = lax.axis_size("segment")
    tiles = lax.axis_size("tile")
    weight = section_weights[0]
    half_rows = weight.shape[0] // 2

    def with_partner(value, d):
        return lax.ppermute(value, "segment", [(s, s ^ d) for s in range(segments)])

    def noise_for(clip):
        return lax.dynamic_index_in_dim(augment_noise[0], clip, 0, keepdims=False)

    order = [3, 1, 2]
    core = tile % 2

    noises = {d: with_partner(noise_for(segment ^ d), d) for d in order}

    weight, noises[order[1]] = lax.optimization_barrier((weight, noises[order[1]]))
    half = lax.dynamic_slice_in_dim(weight, core * half_rows, half_rows, 0)
    halves = {d: with_partner(half, d) for d in order}
    halves[0] = half
    mine = jnp.stack([halves[d] for d in reversed(range(segments))])
    other = on_swap(mine)

    per_step = jnp.concatenate([0.5 * frame_mixing, step_embed])
    flags = jnp.stack(
        [(tile > 0).astype(jnp.int32), (tile < tiles - 1).astype(jnp.int32), 1 - core]
        + [segments - 1 - (segment ^ s) for s in range(segments)]
    )
    start = latent_clips[0].astype(f32)
    noises[order[2]], noises[0], start, per_step, flags = lax.optimization_barrier(
        (noises[order[2]], noise_for(segment), start, per_step, flags)
    )

    def noise_of(section):
        return lax.select_n(segment ^ section, *[noises[d] for d in range(segments)])

    latent = add_noise(start, noise_of(0))
    rows = latent.shape[1]
    late = [noise_of(2), noise_of(3)]
    noise_edges = [
        jnp.concatenate([late[0][:, :2], late[1][:, :1]], axis=1),
        jnp.concatenate([late[0][:, rows - 2 :], late[1][:, rows - 1 :]], axis=1),
    ]
    off_send, on_send = edges_to_send(latent[:, :HALO], latent[:, rows - HALO :])
    off_noise, on_noise = edges_to_send(*noise_edges)
    on, off = on_swap(on_send), off_swap(off_send)
    noise_on, noise_off = on_swap(on_noise), off_swap(off_noise)

    latent, send_off, send_on = run_steps(
        0, (0,) * STEPS_BASE, (None, None, 0), True, flags, latent, off, on, per_step, (mine, other), (noise_of(1),)
    )
    mine, other, latent = lax.optimization_barrier((mine, other, latent))
    off = off_swap(send_off)
    on = on_swap(send_on)
    taps = make_taps(1, segments, flags, mine, other)
    latent = run_steps(
        STEPS_BASE,
        (0, 1, 2),
        (2, 1, None),
        False,
        flags,
        latent,
        off,
        on,
        per_step,
        (taps,),
        (late[0], late[1], noise_on, noise_off),
    )
    return latent[None]


def solution(mesh):
    return jax.shard_map(
        per_device,
        mesh=mesh,
        in_specs=(
            P("segment", None, "tile", None, None),
            P("segment", None, None, "tile", None, None),
            P("segment", None, None),
            P(),
            P(),
        ),
        out_specs=P("segment", None, "tile", None, None),
        check_vma=False,
    )
```

```python
import functools

import jax
import jax.numpy as jnp
from jax import lax
from jax.experimental import pallas as pl
from jax.experimental.pallas import tpu as pltpu
from jax.sharding import PartitionSpec as P

STEPS_BASE = 3
STEPS_SR = 1

norm_eps = 1e-06
keep_coef = 0.9
update_coef = 0.5
noise_coef = 0.5

HALO = 3
CHUNK = 64
SUBLANES = 8
f32 = jnp.float32
bf16 = jnp.bfloat16


def add_noise(latent, noise_piece):
    return (latent.astype(f32) + noise_coef * noise_piece.astype(f32)).astype(bf16)


def fill_taps(taps_ref, weight_ref, start):
    count, chans = weight_ref.shape
    row = taps_ref.shape[0] // 4
    weight = weight_ref[...]
    taps_ref[start : start + count, :chans] = weight
    taps_ref[row + start : row + start + count, chans:] = weight


def build_taps(taps_ref, core, place, mine_ref, other_ref):
    _, half, chans = mine_ref.shape
    row = taps_ref.shape[0] // 4
    taps_ref[3 * row :, :chans] = jnp.zeros((row, chans), bf16)
    taps_ref[:row, chans:] = jnp.zeros((row, chans), bf16)
    for flag, low, high in ((1 - core, mine_ref, other_ref), (core, other_ref, mine_ref)):

        @pl.when(flag == 1)
        def _(low=low, high=high):
            fill_taps(taps_ref, low.at[place], 0)
            fill_taps(taps_ref, high.at[place], half)


def half_place(section):
    return lax.axis_size("segment") - 1 - (lax.axis_index("segment") ^ section)


def taps_kernel(first, mine_ref, other_ref, taps_ref):
    core = lax.axis_index("tile") % 2
    for k in range(taps_ref.shape[0]):
        build_taps(taps_ref.at[k], core, half_place(first + k), mine_ref, other_ref)


def make_taps(first, last, mine, other):
    _, half, chans = mine.shape
    vmem = pl.BlockSpec(memory_space=pltpu.VMEM)
    return pl.pallas_call(
        functools.partial(taps_kernel, first),
        out_shape=jax.ShapeDtypeStruct((last - first, half // 3 * 8, 2 * chans), bf16),
        in_specs=[vmem, vmem],
        out_specs=vmem,
        compiler_params=pltpu.CompilerParams(vmem_limit_bytes=16 * 1024 * 1024),
        cost_estimate=pl.CostEstimate(flops=0, bytes_accessed=(last - first) * half * 16 * chans, transcendentals=0),
    )(mine, other)


def store_mixed(mixed_ref, state_ref, row, mixing, flag):
    frames, _, cols, chans = state_ref.shape
    first, second = [state_ref[frame, row] for frame in range(frames)]
    delta = (second - first) * mixing
    spot = lax.broadcasted_iota(jnp.int32, (SUBLANES, chans), 0)
    for index, mixed in enumerate((first + delta, second - delta)):
        if flag is not None:
            mixed = mixed * flag
        here = pl.ds(index * cols, cols)
        left, right = pltpu.roll(mixed, 1, 0), pltpu.roll(mixed, cols - 1, 0)
        left = jnp.concatenate([jnp.where(spot == 0, 0.0, left[:SUBLANES]), left[SUBLANES:]], axis=0)
        rest = cols - SUBLANES
        right = jnp.concatenate([right[:rest], jnp.where(spot == SUBLANES - 1, 0.0, right[rest:])], axis=0)
        mixed_ref[row, here, :chans] = left.astype(bf16)
        mixed_ref[row, here, chans : 2 * chans] = mixed.astype(bf16)
        mixed_ref[row, here, 2 * chans :] = right.astype(bf16)


def place_halos(even, buffer_ref, off_ref, on_ref, above, below):
    width = off_ref.shape[1]
    for flag, upper, lower in ((even, off_ref, on_ref), (1 - even, on_ref, off_ref)):

        @pl.when(flag == 1)
        def _(upper=upper, lower=lower):
            buffer_ref[:, above : above + width] = upper[...].astype(buffer_ref.dtype)
            buffer_ref[:, below : below + width] = lower[...].astype(buffer_ref.dtype)


def steps_kernel(
    first_step, sections, rows, noise_widths, sends, own_ref, first_ref, second_ref, per_step_ref, *rest
):
    total_rows = rows + 2 * HALO
    rest = list(rest)
    tile = lax.axis_index("tile")
    on_ref, off_ref = (first_ref, second_ref) if sends else (second_ref, first_ref)
    if sends:
        mine_ref, other_ref = rest.pop(0), rest.pop(0)
    else:
        taps_ref = rest.pop(0)
    noises = {k: rest.pop(0) for k, width in enumerate(noise_widths) if width is not None}
    wide = [k for k, width in enumerate(noise_widths) if width]
    if wide:
        noise_off_ref, noise_on_ref = rest.pop(0), rest.pop(0)
    out_ref = rest.pop(0)
    if sends:
        send_off_ref, send_on_ref = rest.pop(0), rest.pop(0)
    state_ref, mixed_ref, conv_ref = rest[:3]
    rest = rest[3:]
    if sends:
        taps_ref = rest.pop(0)
        build_taps(taps_ref.at[0], tile % 2, half_place(0), mine_ref, other_ref)
    else:
        rows_ref, sem = rest.pop(0), rest.pop(0)
    buffers = dict(zip(wide, rest))
    frames, _, cols, chans = own_ref.shape
    up_flag = jnp.where(tile > 0, 1.0, 0.0)
    down_flag = jnp.where(tile < lax.axis_size("tile") - 1, 1.0, 0.0)
    even = 1 - tile % 2
    place_halos(even, state_ref, off_ref, on_ref, 0, HALO + rows)
    start = 0
    for step in wide:
        width = noise_widths[step]
        part = pl.ds(start, width)
        place_halos(
            even, buffers[step], noise_off_ref.at[:, part], noise_on_ref.at[:, part], HALO - width, HALO + rows
        )
        start += width
    def flag_of(row):
        if row < HALO:
            return up_flag
        if row >= HALO + rows:
            return down_flag
        return None

    def is_own(row):
        return HALO <= row < HALO + rows

    def mixing_of(step):
        return per_step_ref[first_step + step : first_step + step + 1, :]

    def first_mix(row):
        if is_own(row):
            for frame in range(frames):
                state_ref[frame, row] = own_ref[frame, row - HALO].astype(f32)
        store_mixed(mixed_ref.at[0], state_ref, row, mixing_of(0), flag_of(row))

    pixels = frames * cols

    def convolve(step, base, slot):
        source = mixed_ref.at[step % 2]
        taps = taps_ref.at[sections[step]]
        for frame in range(frames):
            here = pl.ds(frame * cols, cols)
            patches = jnp.concatenate([source[base + i, here] for i in range(4)], axis=1)
            conv_ref[pl.ds(slot * pixels + frame * cols, cols), :] = jnp.dot(
                patches, taps[...], preferred_element_type=f32
            )

    def update(step, base, slot):
        place = per_step_ref.shape[0] // 2 + first_step + step
        embed = per_step_ref[place : place + 1, :]
        last = step == HALO - 1
        for j in range(2):
            row = base + 1 + j
            for frame in range(frames):
                for spot in range(0, cols, CHUNK):
                    here = pl.ds(spot, CHUNK)
                    part = conv_ref[pl.ds(slot * pixels + frame * cols + spot, CHUNK), j * chans : (j + 1) * chans] + embed
                    mean = jnp.sum(part * part, axis=1, keepdims=True) * (4.0 / chans)
                    half = part * lax.rsqrt(mean + 4.0 * norm_eps)
                    silu = half + half * jnp.tanh(half)
                    new = keep_coef * state_ref[frame, row, here] + update_coef * silu
                    if step in noises:
                        if is_own(row):
                            piece = noises[step][frame, row - HALO, here]
                        else:
                            piece = buffers[step][frame, row, here]
                        new = new + noise_coef * piece.astype(f32)
                    if last:
                        (out_ref if sends else rows_ref)[frame, row - HALO, here] = new.astype(bf16)
                    else:
                        state_ref[frame, row, here] = new
            if last and not sends:
                copy_row(row - HALO).start()
            if not last:
                store_mixed(mixed_ref.at[(step + 1) % 2], state_ref, row, mixing_of(step + 1), flag_of(row))

    def copy_row(row):
        return pltpu.make_async_copy(rows_ref.at[:, row], out_ref.at[:, row], sem.at[row])

    waiting = None
    mixed_rows = 0
    slot = 0
    for step in range(HALO):
        for base in range(step, total_rows - step - 2, 2):
            if step == 0:
                while mixed_rows < base + 4:
                    first_mix(mixed_rows)
                    mixed_rows += 1
            convolve(step, base, slot)
            if waiting is not None:
                update(*waiting)
            waiting = (step, base, slot)
            slot = 1 - slot
    update(*waiting)
    if not sends:
        for row in range(rows):
            copy_row(row).wait()
    if sends:
        for flag, off_rows, on_rows in ((even, 0, rows - HALO), (1 - even, rows - HALO, 0)):

            @pl.when(flag == 1)
            def _(off_rows=off_rows, on_rows=on_rows):
                send_off_ref[...] = out_ref[:, off_rows : off_rows + HALO]
                send_on_ref[...] = out_ref[:, on_rows : on_rows + HALO]


def run_steps(first_step, sections, noise_widths, sends, own, off, on, per_step, taps, noises):
    frames, rows, cols, chans = own.shape
    depth = 9 * chans
    total = rows + 2 * HALO
    vmem = pl.BlockSpec(memory_space=pltpu.VMEM)
    halos = (on, off) if sends else (off, on)
    operands = (own, *halos, per_step, *taps, *noises)
    outputs = sum(total - 2 * (k + 1) for k in range(HALO)) * frames * cols
    state = pltpu.VMEM((frames, total, cols, chans), f32)
    edges = pltpu.VMEM((frames, total, cols, chans), bf16)
    edge = jax.ShapeDtypeStruct((frames, HALO, cols, chans), bf16)
    whole = jax.ShapeDtypeStruct(own.shape, bf16)
    return pl.pallas_call(
        functools.partial(steps_kernel, first_step, sections, rows, noise_widths, sends),
        out_shape=(whole, edge, edge) if sends else whole,
        in_specs=[vmem] * len(operands),
        out_specs=(vmem, vmem, vmem) if sends else pl.BlockSpec(memory_space=pl.ANY),
        scratch_shapes=[
            state,
            pltpu.VMEM((2, total, frames * cols, 3 * chans), bf16),
            pltpu.VMEM((2 * frames * cols, 2 * chans), f32),
        ]
        + (
            [pltpu.VMEM((1, depth // 3 * 4, 2 * chans), bf16)]
            if sends
            else [pltpu.VMEM(own.shape, bf16), pltpu.SemaphoreType.DMA((rows,))]
        )
        + [edges for width in noise_widths if width],
        compiler_params=pltpu.CompilerParams(vmem_limit_bytes=40 * 1024 * 1024),
        cost_estimate=pl.CostEstimate(
            flops=2 * outputs * depth * chans, bytes_accessed=4 * own.size, transcendentals=outputs * chans
        ),
    )(*operands)


def off_swap(value):
    count = lax.axis_size("tile")
    return lax.ppermute(value, "tile", [p for i in range(1, count - 1, 2) for p in ((i, i + 1), (i + 1, i))])


def on_swap(value):
    return lax.ppermute(value, "tile", [(i, i ^ 1) for i in range(lax.axis_size("tile"))])


def edges_to_send(top, bottom):
    even = lax.axis_index("tile") % 2 == 0
    return jnp.where(even, top, bottom), jnp.where(even, bottom, top)


def per_device(latent_clips, augment_noise, section_weights, frame_mixing, step_embed):
    segment = lax.axis_index("segment")
    tile = lax.axis_index("tile")
    segments = lax.axis_size("segment")
    tiles = lax.axis_size("tile")
    weight = section_weights[0]
    half_rows = weight.shape[0] // 2

    def with_partner(value, d):
        return lax.ppermute(value, "segment", [(s, s ^ d) for s in range(segments)])

    def noise_for(clip):
        return lax.dynamic_index_in_dim(augment_noise[0], clip, 0, keepdims=False)

    order = [3, 1, 2]
    core = tile % 2

    noises = {d: with_partner(noise_for(segment ^ d), d) for d in order}

    weight, noises[order[1]] = lax.optimization_barrier((weight, noises[order[1]]))
    half = lax.dynamic_slice_in_dim(weight, core * half_rows, half_rows, 0)
    halves = {d: with_partner(half, d) for d in order}
    halves[0] = half
    mine = jnp.stack([halves[d] for d in reversed(range(segments))])
    other = on_swap(mine)

    per_step = jnp.concatenate([0.5 * frame_mixing, step_embed])
    start = latent_clips[0].astype(f32)
    noises[order[2]], noises[0], start, per_step = lax.optimization_barrier(
        (noises[order[2]], noise_for(segment), start, per_step)
    )

    def noise_of(section):
        return lax.select_n(segment ^ section, *[noises[d] for d in range(segments)])

    latent = add_noise(start, noise_of(0))
    rows = latent.shape[1]
    late = [noise_of(2), noise_of(3)]
    noise_edges = [
        jnp.concatenate([late[0][:, :2], late[1][:, :1]], axis=1),
        jnp.concatenate([late[0][:, rows - 2 :], late[1][:, rows - 1 :]], axis=1),
    ]
    off_send, on_send = edges_to_send(latent[:, :HALO], latent[:, rows - HALO :])
    off_noise, on_noise = edges_to_send(*noise_edges)
    on, off = on_swap(on_send), off_swap(off_send)
    noise_on, noise_off = on_swap(on_noise), off_swap(off_noise)

    latent, send_off, send_on = run_steps(
        0, (0,) * STEPS_BASE, (None, None, 0), True, latent, off, on, per_step, (mine, other), (noise_of(1),)
    )
    mine, other, latent = lax.optimization_barrier((mine, other, latent))
    off = off_swap(send_off)
    on = on_swap(send_on)
    taps = make_taps(1, segments, mine, other)
    latent = run_steps(
        STEPS_BASE,
        (0, 1, 2),
        (2, 1, None),
        False,
        latent,
        off,
        on,
        per_step,
        (taps,),
        (late[0], late[1], noise_off, noise_on),
    )
    return latent[None]


def solution(mesh):
    return jax.shard_map(
        per_device,
        mesh=mesh,
        in_specs=(
            P("segment", None, "tile", None, None),
            P("segment", None, None, "tile", None, None),
            P("segment", None, None),
            P(),
            P(),
        ),
        out_specs=P("segment", None, "tile", None, None),
        check_vma=False,
    )
```
